128 devices in a mesh: section: 4 (over x), expert: 32 (over z, y, core).
Axes of the slice: x: 4, y: 4, z: 4, core: 2. Of those that a mesh axis runs over, the one named last changes fastest.
Arguments:
- stash: bfloat16 [4, 4096, 4096], P('section', 'expert'), may hold values from -6 to 6
- out_grad: bfloat16 [4, 4096, 4096], P('section', 'expert'), may hold values from -6 to 6
- expert_ids: int32 [4, 4096, 1], P('section', 'expert'), may hold values from 0 to 7; in each aligned block of 128 rows (0 to 127, 128 to 255, ..., all dimensions but the last counted through in order) at most 24 rows name the same one
- gate_probs: float32 [4, 4096, 1], P('section', 'expert'), may hold values from 0.05 to 1
- w_gate: bfloat16 [4, 32, 4096, 384], P('section', 'expert'), may hold values from -0.09375 to 0.09375
- w_up: bfloat16 [4, 32, 4096, 384], P('section', 'expert'), may hold values from -0.09375 to 0.09375
- w_down: bfloat16 [4, 32, 384, 4096], P('section', 'expert'), may hold values from -0.15625 to 0.15625
Outputs:
- prev_grad: bfloat16 [4, 4096, 4096], P('section', 'expert')
- grad_gate: bfloat16 [4, 32, 4096, 384], P('section', 'expert')
- grad_up: bfloat16 [4, 32, 4096, 384], P('section', 'expert')
- grad_down: bfloat16 [4, 32, 384, 4096], P('section', 'expert')
The draws below stay inside these ranges and needn't reach their ends.
Inputs may be any that keep to these rules, and one draw needn't show every extreme that they name: `expert_ids`: among the 128 tokens of one device (aligned blocks of rows of one layer), no expert is named more than 24 times; in every draw some expert is named exactly 24 times by the tokens of some device. Each token chooses exactly one expert.
All inputs are finite; a program needn't handle non-finite values.
Results may differ from the reference program's by a relative error of at most 0.0058.
Values may be sent and summed in bfloat16 or wider, within the bound.
No kernel may reach another device: no remote copies, remote signals or barrier semaphores. Data moves between devices by JAX's collectives and lax.ppermute only.
A program may use at most 192 MiB of HBM per device.

```python
import math
import jax
import jax.numpy as jnp
import numpy as np
from jax import lax

D = 4096
H = 1536
SPLIT = 4
HS = 384
TOP = 1
EXPERTS = 8
SHARDS = 32
SECTIONS = 4
TOK_DEV = 128
TOKENS = 4096
CAP = 24
N_EXPERT = 32


def shard_levels(own_key, shape, cuts, least, largest):
    factor_of, own = 1.0, jax.random.fold_in(own_key, 6)
    for position, blocks in cuts:
        heights = jnp.exp(jax.random.uniform(jax.random.fold_in(own, position), (blocks,), jnp.float32, least / len(cuts), largest / len(cuts)))
        factor_of = factor_of * jnp.repeat(heights, shape[position] // blocks).reshape([-1 if axis == position else 1 for axis in range(len(shape))])
    return factor_of


def deal_out(key, own, number, rows, count, top, reach, slope):
    sequence = jax.random.permutation(key, count)
    packed, ordinary = shares(count, rows * top, reach, slope, True), shares(count, rows * top, reach, slope, False)
    places = jnp.arange(count)

    def named(sizes, offset_by):
        used = int((sizes > 0).sum())
        fixed = max(1, used // 4)
        shifted = fixed + (places - fixed + offset_by * (used - fixed)) % max(1, count - fixed)
        return jnp.zeros((count,), jnp.int32).at[sequence[jnp.where(places < fixed, places, shifted)]].set(jnp.asarray(sizes, jnp.int32))

    sizes = jnp.where(number % 4 == 0, named(packed, number // 4), named(ordinary, number - number // 4 - 1))
    mixed = jax.random.permutation(jax.random.fold_in(own, 3), count)
    source_of, taker = mixed[0:count // 2 * 2:2], mixed[1:count // 2 * 2:2]
    margin = jnp.minimum(sizes[source_of] - 1, reach - sizes[taker]) // 2
    margin = jnp.where((source_of == sequence[0]) | (taker == sequence[0]) | (sizes[taker] == 0), 0, jnp.maximum(margin, 0))
    shifted = jax.random.randint(jax.random.fold_in(own, 4), (count // 2,), 0, 1 << 20) % (margin + 1)
    sizes = sizes.at[source_of].add(-shifted).at[taker].add(shifted)
    labels = jnp.searchsorted(jnp.cumsum(sizes), jnp.arange(rows * top), side="right").astype(jnp.int32)
    grid = labels.reshape(top, rows).T
    grid = grid[jax.random.permutation(jax.random.fold_in(own, 1), rows)]
    offset_by = jax.random.randint(jax.random.fold_in(own, 2), (rows, 1), 0, top)
    return jnp.take_along_axis(grid, (jnp.arange(top)[None, :] + offset_by) % top, axis=1)


def shares(amount, total, reach, slope, full):
    weights = [(1 << 20) // math.isqrt(grade ** slope) + 1 for grade in range(1, amount + 1)]
    largest = reach if full else min(reach, max(-(-total // amount), total * weights[0] // sum(weights)))
    least = 1 if total - largest >= amount - 1 else 0
    given, rest = [largest] + [least] * (amount - 1), total - largest - least * (amount - 1)
    while rest > 0:
        candidates = [i for i in range(1, amount) if given[i] < largest] or [i for i in range(1, amount) if given[i] < reach]
        pool, remaining = sum([weights[i] for i in candidates]), rest
        for i in candidates:
            extra = min(reach - given[i], max(1, remaining * weights[i] // pool), rest)
            given[i] = given[i] + extra
            rest = rest - extra
    return np.array(given)


def centred(own_key, dims, width, limit, cuts=(), kind=jnp.bfloat16):
    result = jax.random.normal(own_key, dims, jnp.float32) * width
    if len(cuts) > 0:
        result = shard_levels(own_key, dims, cuts, -0.22, 0.18) * result
    return jnp.clip(result, min=-limit, max=limit).astype(kind)


def setup_inputs(seed: int = 0) -> dict:
    key_list = jax.random.split(jax.random.key(seed), 8)
    stash = centred(key_list[0], (SECTIONS, TOKENS, D), 1.0, 6.0, ((0, 4), (1, 32)))
    out_grad = centred(key_list[1], (SECTIONS, TOKENS, D), 1.0, 6.0, ((0, 4), (1, 32)))
    expert_ids_keys = jax.random.split(jax.random.fold_in(key_list[2], 1), SECTIONS * TOKENS // TOK_DEV)
    expert_ids_turns = jax.random.permutation(jax.random.fold_in(key_list[2], 3), SECTIONS * TOKENS // TOK_DEV)
    expert_ids = jax.vmap(lambda own, number: deal_out(jax.random.fold_in(key_list[2], 2), own, number, TOK_DEV, EXPERTS, TOP, CAP, 2))(expert_ids_keys, expert_ids_turns).reshape((SECTIONS, TOKENS, TOP))
    gate_probs = jnp.clip(jnp.exp(math.log(1.0) - 2.9957323 * jax.random.uniform(key_list[3], (SECTIONS, TOKENS, TOP), jnp.float32) ** shard_levels(key_list[3], (SECTIONS, TOKENS, TOP), ((0, 4), (1, 32)), -0.2, 0.2)), 0.05, 1.0)
    w_gate = centred(key_list[4], (SECTIONS, SHARDS, D, HS), D ** -0.5, 0.09375, ((0, 4), (1, 32)))
    w_up = centred(key_list[5], (SECTIONS, SHARDS, D, HS), D ** -0.5, 0.09375, ((0, 4), (1, 32)))
    w_down = centred(key_list[6], (SECTIONS, SHARDS, HS, D), H ** -0.5, 0.15625, ((0, 4), (1, 32)))
    return {"stash": stash, "out_grad": out_grad, "expert_ids": expert_ids, "gate_probs": gate_probs, "w_gate": w_gate, "w_up": w_up, "w_down": w_down}


def contract(left, right, left_dim, right_dim):
    return lax.dot_general(left, right, (((left_dim,), (right_dim,)), ((), ())), preferred_element_type=jnp.float32)


def expert_grads(operands):
    token_rows, grad_rows, gate_weight, up_weight, down_weight = operands
    gate_pre = contract(token_rows, gate_weight, 1, 0)
    up_pre = contract(token_rows, up_weight, 1, 0)
    sigmoid_a = jax.nn.sigmoid(gate_pre)
    silu_a = gate_pre * sigmoid_a
    hidden = (silu_a * up_pre).astype(jnp.bfloat16)
    grad_down = contract(hidden, grad_rows, 0, 0).astype(jnp.bfloat16)
    hidden_grad = contract(grad_rows, down_weight, 1, 1)
    gate_delta = (hidden_grad * up_pre * sigmoid_a * (1.0 + gate_pre * (1.0 - sigmoid_a))).astype(jnp.bfloat16)
    up_delta = (hidden_grad * silu_a).astype(jnp.bfloat16)
    grad_gate = contract(token_rows, gate_delta, 0, 0).astype(jnp.bfloat16)
    grad_up = contract(token_rows, up_delta, 0, 0).astype(jnp.bfloat16)
    row_grads = contract(gate_delta, gate_weight, 1, 1) + contract(up_delta, up_weight, 1, 1)
    return row_grads, grad_gate, grad_up, grad_down


def section_grads(operands):
    stash, out_grad, expert_ids, gate_probs, w_gate, w_up, w_down = operands
    pair_ids = expert_ids.reshape(N_EXPERT, TOK_DEV * TOP).astype(jnp.int32)
    onehot = (pair_ids[:, :, None] == jnp.arange(EXPERTS, dtype=jnp.int32)[None, None, :]).astype(jnp.int32)
    slot_rank = jnp.sum((jnp.cumsum(onehot, axis=1) - onehot) * onehot, axis=2)
    source = jnp.arange(N_EXPERT, dtype=jnp.int32)[:, None]
    slot_index = ((pair_ids * N_EXPERT + source) * CAP + slot_rank).reshape(-1).astype(jnp.int32)
    token_of = (jnp.arange(TOKENS * TOP, dtype=jnp.int32) // TOP).astype(jnp.int32)
    scaled = (gate_probs[:, :, None] * out_grad[:, None, :].astype(jnp.float32)).astype(jnp.bfloat16)
    scaled = scaled.reshape(TOKENS * TOP, D)
    slot_count = EXPERTS * N_EXPERT * CAP
    token_buf = jnp.zeros((slot_count, D), jnp.bfloat16).at[slot_index].set(stash[token_of])
    grad_buf = jnp.zeros((slot_count, D), jnp.bfloat16).at[slot_index].set(scaled)
    token_buf = token_buf.reshape(EXPERTS, N_EXPERT * CAP, D)
    grad_buf = grad_buf.reshape(EXPERTS, N_EXPERT * CAP, D)
    gate_full = w_gate.reshape(EXPERTS, SPLIT, D, HS).transpose(0, 2, 1, 3).reshape(EXPERTS, D, H)
    up_full = w_up.reshape(EXPERTS, SPLIT, D, HS).transpose(0, 2, 1, 3).reshape(EXPERTS, D, H)
    down_full = w_down.reshape(EXPERTS, H, D)
    row_grads, grad_gate, grad_up, grad_down = lax.map(expert_grads, (token_buf, grad_buf, gate_full, up_full, down_full))
    pair_grads = row_grads.reshape(slot_count, D)[slot_index].reshape(TOKENS, TOP, D)
    input_grad = jnp.sum(pair_grads, axis=1).astype(jnp.bfloat16)
    grad_gate = grad_gate.reshape(EXPERTS, D, SPLIT, HS).transpose(0, 2, 1, 3).reshape(SHARDS, D, HS)
    grad_up = grad_up.reshape(EXPERTS, D, SPLIT, HS).transpose(0, 2, 1, 3).reshape(SHARDS, D, HS)
    grad_down = grad_down.reshape(SHARDS, HS, D)
    return input_grad, grad_gate, grad_up, grad_down


def reference(stash, out_grad, expert_ids, gate_probs, w_gate, w_up, w_down):
    input_grad, grad_gate, grad_up, grad_down = lax.map(section_grads, (stash, out_grad, expert_ids, gate_probs, w_gate, w_up, w_down))
    return jnp.roll(input_grad, -1, axis=0), grad_gate, grad_up, grad_down
```

```python
import jax
import jax.numpy as jnp
import numpy as np
from jax import lax
from jax.sharding import Mesh, PartitionSpec as P

SPLIT = 4
CORES = 2


def contract(left, right, left_dim, right_dim):
    return lax.dot_general(
        left, right, (((left_dim,), (right_dim,)), ((), ())), preferred_element_type=jnp.float32
    )


def swap_cores(value):
    return lax.ppermute(value, "core", [(0, 1), (1, 0)])


def over_chips(value):
    return lax.all_to_all(value, "chip", split_axis=0, concat_axis=0, tiled=True)


def body(stash, out_grad, expert_ids, gate_probs, w_gate, w_up, w_down):
    chips = lax.axis_size("chip")
    sections = lax.axis_size("section")
    tokens, width = stash.shape[1], stash.shape[2]
    experts = chips * CORES // SPLIT
    halves = SPLIT // CORES
    capacity = tokens * 3 // (2 * experts)
    slots = experts * capacity
    routed = expert_ids[0].reshape(-1)
    onehot = (routed[:, None] == jnp.arange(experts, dtype=jnp.int32)[None, :]).astype(jnp.int32)
    rank = jnp.sum((jnp.cumsum(onehot, axis=0) - onehot) * onehot, axis=1)
    slot = routed * capacity + rank
    place = (jnp.arange(slots, dtype=jnp.int32)[:, None] == slot[None, :]).astype(jnp.bfloat16)
    scaled = (gate_probs[0] * out_grad[0].astype(jnp.float32)).astype(jnp.bfloat16)

    def deal(rows):
        packed = contract(place, rows, 1, 0).astype(jnp.bfloat16)
        packed = packed.reshape(experts, 1, capacity, width)
        copies = jnp.broadcast_to(packed, (experts, halves, capacity, width))
        return copies.reshape(chips, capacity, width)

    mine = over_chips(jnp.concatenate([deal(stash[0]), deal(scaled)], axis=2))
    other = swap_cores(mine)
    rows = chips * capacity
    both = jnp.concatenate([mine, other], axis=0).reshape(2 * rows, 2 * width)
    token_rows, grad_rows = both[:, :width], both[:, width:]
    wg, wu, wd = w_gate[0, 0], w_up[0, 0], w_down[0, 0]
    gate_pre = contract(token_rows, wg, 1, 0)
    up_pre = contract(token_rows, wu, 1, 0)
    sigmoid_a = jax.nn.sigmoid(gate_pre)
    silu_a = gate_pre * sigmoid_a
    hidden = (silu_a * up_pre).astype(jnp.bfloat16)
    hidden_grad = contract(grad_rows, wd, 1, 1)
    gate_delta = (hidden_grad * up_pre * sigmoid_a * (1.0 + gate_pre * (1.0 - sigmoid_a))).astype(
        jnp.bfloat16
    )
    up_delta = (hidden_grad * silu_a).astype(jnp.bfloat16)
    row_grads = contract(gate_delta, wg, 1, 1) + contract(up_delta, wu, 1, 1)
    theirs = swap_cores(row_grads[rows:].astype(jnp.bfloat16))
    back = (row_grads[:rows] + theirs.astype(jnp.float32)).astype(jnp.bfloat16)
    returned = over_chips(back.reshape(chips, capacity, width))
    returned = returned.reshape(experts, halves, capacity, width)
    place_back = jnp.broadcast_to(
        place.reshape(experts, 1, capacity, tokens), (experts, halves, capacity, tokens)
    ).reshape(experts * halves * capacity, tokens)
    input_grad = contract(
        place_back, returned.reshape(experts * halves * capacity, width), 0, 0
    ).astype(jnp.bfloat16)
    prev_grad = lax.ppermute(
        input_grad, "section", [(i, (i - 1) % sections) for i in range(sections)]
    )
    grad_down = contract(hidden, grad_rows, 0, 0).astype(jnp.bfloat16)
    grad_gate = contract(token_rows, gate_delta, 0, 0).astype(jnp.bfloat16)
    grad_up = contract(token_rows, up_delta, 0, 0).astype(jnp.bfloat16)
    return (prev_grad[None], grad_gate[None, None], grad_up[None, None], grad_down[None, None])


def solution(mesh):
    sections, devices = mesh.devices.shape
    fine = Mesh(mesh.devices.reshape(sections, devices // CORES, CORES), ("section", "chip", "core"))
    spec = P("section", ("chip", "core"))
    return jax.shard_map(
        body, mesh=fine, in_specs=(spec,) * 7, out_specs=(spec,) * 4, check_vma=False
    )
```

```python
import jax
import jax.numpy as jnp
from jax import lax
from jax.sharding import Mesh, PartitionSpec as P

SPLIT = 4
CORES = 2
RING = 4
GROUPS = (
    ((2, 1), (1, 2), (2, 3), (3, 2)),
    ((1, 1), (3, 3), (1, 3), (3, 1)),
    ((2, 2), (0, 2), (2, 0)),
    ((0, 1), (1, 0), (0, 3), (3, 0), (0, 0)),
)
PARTS = 2


def contract(left, right, left_dim, right_dim):
    return lax.dot_general(
        left, right, (((left_dim,), (right_dim,)), ((), ())), preferred_element_type=jnp.float32
    )


def swap_cores(value):
    return lax.ppermute(value, "core", [(0, 1), (1, 0)])


def offset_of(chip, offset):
    z, y = chip // RING, chip % RING
    return (z + offset[0]) % RING * RING + (y + offset[1]) % RING


def send(value, offset, sign):
    if offset == (0, 0):
        return value
    step = (sign * offset[0], sign * offset[1])
    return lax.ppermute(value, "chip", [(i, offset_of(i, step)) for i in range(RING * RING)])


def body(stash, out_grad, expert_ids, gate_probs, w_gate, w_up, w_down):
    chips = lax.axis_size("chip")
    sections = lax.axis_size("section")
    tokens, width = stash.shape[1], stash.shape[2]
    hidden_width = w_gate.shape[3]
    experts = chips * CORES // SPLIT
    halves = SPLIT // CORES
    capacity = tokens * 3 // (2 * experts)
    chip = lax.axis_index("chip")
    routed = expert_ids[0].reshape(-1)
    onehot = (routed[:, None] == jnp.arange(experts, dtype=jnp.int32)[None, :]).astype(jnp.int32)
    rank = jnp.sum((jnp.cumsum(onehot, axis=0) - onehot) * onehot, axis=1)
    slot = routed * capacity + rank
    scaled = (gate_probs[0] * out_grad[0].astype(jnp.float32)).astype(jnp.bfloat16)
    paired = jnp.concatenate([stash[0], scaled], axis=1)
    both_weights = jnp.concatenate([w_gate[0, 0], w_up[0, 0]], axis=1)
    down_weight = w_down[0, 0]

    places = {}
    dealt = {}
    for group in GROUPS:
        for offset in group:
            expert = offset_of(chip, offset) // halves
            wanted = expert * capacity + jnp.arange(capacity, dtype=jnp.int32)
            places[offset] = (wanted[:, None] == slot[None, :]).astype(jnp.bfloat16)
            rows = contract(places[offset], paired, 1, 0).astype(jnp.bfloat16)
            dealt[offset] = send(rows, offset, 1)

    token_parts, grad_parts, hidden_parts, delta_parts = [], [], [], []
    returned = [{} for _ in range(PARTS)]
    span = width // PARTS
    for group in GROUPS:
        mine = jnp.concatenate([dealt[offset] for offset in group], axis=0)
        count = mine.shape[0]
        both = jnp.concatenate([mine, swap_cores(mine)], axis=0)
        token_rows, grad_rows = both[:, :width], both[:, width:]
        pre = contract(token_rows, both_weights, 1, 0)
        gate_pre, up_pre = pre[:, :hidden_width], pre[:, hidden_width:]
        sigmoid_a = jax.nn.sigmoid(gate_pre)
        silu_a = gate_pre * sigmoid_a
        hidden = (silu_a * up_pre).astype(jnp.bfloat16)
        hidden_grad = contract(grad_rows, down_weight, 1, 1)
        gate_delta = (
            hidden_grad * up_pre * sigmoid_a * (1.0 + gate_pre * (1.0 - sigmoid_a))
        ).astype(jnp.bfloat16)
        up_delta = (hidden_grad * silu_a).astype(jnp.bfloat16)
        deltas = jnp.concatenate([gate_delta, up_delta], axis=1)
        for part in range(PARTS):
            weights = both_weights[part * span : (part + 1) * span]
            theirs = contract(deltas[count:], weights, 1, 1).astype(jnp.bfloat16)
            ours = contract(deltas[:count], weights, 1, 1)
            back = (ours + swap_cores(theirs).astype(jnp.float32)).astype(jnp.bfloat16)
            for i, offset in enumerate(group):
                rows = back[i * capacity : (i + 1) * capacity]
                returned[part][offset] = send(rows, offset, -1)
        token_parts.append(token_rows)
        grad_parts.append(grad_rows)
        hidden_parts.append(hidden)
        delta_parts.append(deltas)

    order = [offset for group in GROUPS for offset in group]
    place_all = jnp.concatenate([places[offset] for offset in order], axis=0)
    prev_parts = []
    for part in range(PARTS):
        rows = jnp.concatenate([returned[part][offset] for offset in order], axis=0)
        input_grad = contract(place_all, rows, 0, 0).astype(jnp.bfloat16)
        prev_parts.append(
            lax.ppermute(
                input_grad, "section", [(i, (i - 1) % sections) for i in range(sections)]
            )
        )
    prev_grad = jnp.concatenate(prev_parts, axis=1)
    token_rows = jnp.concatenate(token_parts, axis=0)
    grad_rows = jnp.concatenate(grad_parts, axis=0)
    hidden = jnp.concatenate(hidden_parts, axis=0)
    deltas = jnp.concatenate(delta_parts, axis=0)
    grad_down = contract(hidden, grad_rows, 0, 0).astype(jnp.bfloat16)
    grad_gate = contract(token_rows, deltas[:, :hidden_width], 0, 0).astype(jnp.bfloat16)
    grad_up = contract(token_rows, deltas[:, hidden_width:], 0, 0).astype(jnp.bfloat16)
    return (prev_grad[None], grad_gate[None, None], grad_up[None, None], grad_down[None, None])


def solution(mesh):
    sections, devices = mesh.devices.shape
    fine = Mesh(mesh.devices.reshape(sections, devices // CORES, CORES), ("section", "chip", "core"))
    spec = P("section", ("chip", "core"))
    return jax.shard_map(
        body, mesh=fine, in_specs=(spec,) * 7, out_specs=(spec,) * 4, check_vma=False
    )
```

```python
import functools

import jax
import jax.numpy as jnp
from jax import lax
from jax.experimental import pallas as pl
from jax.experimental.pallas import tpu as pltpu
from jax.sharding import Mesh, PartitionSpec as P

SPLIT = 4
CORES = 2
HALVES = SPLIT // CORES
MIB = 1 << 20
LIMIT = 56 * MIB
NEXT_LAST = (((1,), (1,)), ((), ()))
FIRST_FIRST = (((0,), (0,)), ((), ()))


def dot(left, right, dims=(((1,), (0,)), ((), ()))):
    return lax.dot_general(left, right, dims, preferred_element_type=jnp.float32)


def swap_cores(value):
    return lax.ppermute(value, "core", [(0, 1), (1, 0)])


def over_chips(value):
    return lax.all_to_all(value, "chip", split_axis=0, concat_axis=0, tiled=True)


def cost(flops, moved):
    return pl.CostEstimate(flops=flops, bytes_accessed=moved, transcendentals=0)


def places(ids, rank, chunks, experts, slot_dim, shape):
    found = []
    at = 0
    for depth in chunks:
        slot = lax.broadcasted_iota(jnp.int32, shape(experts * HALVES * depth), slot_dim)
        inside = (rank >= at) & (rank < at + depth)
        first = ids * (HALVES * depth) + rank - at
        hit = (slot == first) | (slot == first + depth)
        found.append((hit & inside).astype(jnp.float32).astype(jnp.bfloat16))
        at += depth
    return found


def deal_kernel(experts, chunks, blocks, row_ids, col_ids, gates, stash, out_grad, *refs):
    number = len(chunks)
    dealt, place_back, place = refs[:number], refs[number : 2 * number], refs[2 * number :]
    step = pl.program_id(0)
    tokens = col_ids.shape[0]

    @pl.when(step == 0)
    def _():
        first = lax.broadcasted_iota(jnp.int32, (tokens, tokens), 0)
        second = lax.broadcasted_iota(jnp.int32, (tokens, tokens), 1)
        ids = row_ids[...]
        hot = (lax.broadcasted_iota(jnp.int32, (experts, tokens), 0) == ids).astype(jnp.float32)
        before = dot(hot.astype(jnp.bfloat16), (first < second).astype(jnp.bfloat16))
        rank = jnp.sum(before * hot, axis=0, keepdims=True).astype(jnp.int32)
        found = places(ids, rank, chunks, experts, 0, lambda slots: (slots, tokens))
        for ref, value in zip(place, found):
            ref[...] = value
        ids = col_ids[...]
        hot = (lax.broadcasted_iota(jnp.int32, (tokens, experts), 1) == ids).astype(jnp.float32)
        before = dot((second < first).astype(jnp.bfloat16), hot.astype(jnp.bfloat16))
        rank = jnp.sum(before * hot, axis=1, keepdims=True).astype(jnp.int32)
        found = places(ids, rank, chunks, experts, 1, lambda slots: (tokens, slots))
        for ref, value in zip(place_back, found):
            ref[...] = value

    @pl.when(step < blocks)
    def _():
        for ref, at in zip(dealt, place):
            ref[...] = dot(at[...], stash[...]).astype(jnp.bfloat16)

    @pl.when(step >= blocks)
    def _():
        scaled = (gates[...] * out_grad[...].astype(jnp.float32)).astype(jnp.bfloat16)
        for ref, at in zip(dealt, place):
            ref[...] = dot(at[...], scaled).astype(jnp.bfloat16)


def deal(ids, gates, stash, out_grad, experts, chunks):
    tokens, width = stash.shape
    slots = [experts * HALVES * depth for depth in chunks]
    blocks = 4
    span = width // blocks
    outs = pl.pallas_call(
        functools.partial(deal_kernel, experts, chunks, blocks),
        grid=(2 * blocks,),
        in_specs=[
            pl.BlockSpec((1, tokens), lambda i: (0, 0)),
            pl.BlockSpec((tokens, 1), lambda i: (0, 0)),
            pl.BlockSpec((tokens, 1), lambda i: (0, 0)),
            pl.BlockSpec((tokens, span), lambda i: (0, jnp.minimum(i, blocks - 1))),
            pl.BlockSpec((tokens, span), lambda i: (0, jnp.maximum(i - blocks, 0))),
        ],
        out_specs=[pl.BlockSpec((count, span), lambda i: (0, i)) for count in slots]
        + [pl.BlockSpec((tokens, count), lambda i: (0, 0)) for count in slots],
        out_shape=[jax.ShapeDtypeStruct((count, 2 * width), jnp.bfloat16) for count in slots]
        + [jax.ShapeDtypeStruct((tokens, count), jnp.bfloat16) for count in slots],
        scratch_shapes=[pltpu.VMEM((count, tokens), jnp.bfloat16) for count in slots],
        compiler_params=pltpu.CompilerParams(vmem_limit_bytes=LIMIT),
        cost_estimate=cost(4 * sum(slots) * tokens * width, 6 * sum(slots) * width),
        name="deal_rows",
    )(ids.reshape(1, tokens), ids, gates, stash, out_grad)
    return outs[: len(chunks)], outs[len(chunks) :]


def middle_kernel(steps, rows_ref, go, uo, do, gs, us, ds, back, hidden, deltas, *scratch):
    held, joined, down, pre, tail, sems = scratch
    rows, width = back.shape
    units = go.shape[1]
    span = width // steps

    def copies(k):
        at = pl.ds(pl.multiple_of(k * span, span), span)
        late = pl.ds(pl.multiple_of(width + k * span, span), span)
        pairs = [
            (rows_ref.at[:, at], held.at[:, at]),
            (rows_ref.at[:, late], held.at[:, late]),
            (do.at[:, at], down.at[pl.ds(0, units), at]),
            (ds.at[:, at], down.at[pl.ds(units, units), at]),
        ]
        for i, weight in enumerate((go, uo, gs, us)):
            pairs.append((weight.at[at, :], joined.at[at, pl.ds(i * units, units)]))
        return [
            pltpu.make_async_copy(src, dst, sems.at[i, k]) for i, (src, dst) in enumerate(pairs)
        ]

    @pl.loop(0, steps)
    def _(k):
        for copy in copies(k):
            copy.start()

    pre[...] = jnp.zeros_like(pre)
    tail[...] = jnp.zeros_like(tail)

    @pl.loop(0, steps)
    def _(k):
        for copy in copies(k):
            copy.wait()
        at = pl.ds(pl.multiple_of(k * span, span), span)
        late = pl.ds(pl.multiple_of(width + k * span, span), span)
        pre[...] += dot(held[:, at], joined[at, :])
        tail[...] += dot(held[:, late], down[:, at], NEXT_LAST)

    @pl.loop(0, rows // 16)
    def _(r):
        at = pl.ds(pl.multiple_of(r * 16, 16), 16)
        for core in range(CORES):
            gate = slice(2 * core * units, (2 * core + 1) * units)
            up = slice((2 * core + 1) * units, (2 * core + 2) * units)
            own = slice(core * units, (core + 1) * units)
            gate_pre, up_pre, grad = pre[at, gate], pre[at, up], tail[at, own]
            sigmoid_a = jax.nn.sigmoid(gate_pre)
            silu_a = gate_pre * sigmoid_a
            hidden[at, own] = (silu_a * up_pre).astype(jnp.bfloat16)
            deltas[at, gate] = (
                grad * up_pre * sigmoid_a * (1.0 + gate_pre * (1.0 - sigmoid_a))
            ).astype(jnp.bfloat16)
            deltas[at, up] = (grad * silu_a).astype(jnp.bfloat16)

    @pl.loop(0, steps)
    def _(k):
        at = pl.ds(pl.multiple_of(k * span, span), span)
        back[:, at] = dot(deltas[...], joined[at, :], NEXT_LAST).astype(jnp.bfloat16)


def middle(rows, own, sibling):
    count, width = rows.shape[0], rows.shape[1] // 2
    units = own[0].shape[1]
    steps = 4
    anywhere = pl.BlockSpec(memory_space=pl.ANY)
    whole = pl.BlockSpec(memory_space=pltpu.VMEM)
    return pl.pallas_call(
        functools.partial(middle_kernel, steps),
        in_specs=[anywhere] * 7,
        out_specs=[whole] * 3,
        out_shape=[
            jax.ShapeDtypeStruct((count, width), jnp.bfloat16),
            jax.ShapeDtypeStruct((count, CORES * units), jnp.bfloat16),
            jax.ShapeDtypeStruct((count, 2 * CORES * units), jnp.bfloat16),
        ],
        scratch_shapes=[
            pltpu.VMEM((count, 2 * width), jnp.bfloat16),
            pltpu.VMEM((width, 2 * CORES * units), jnp.bfloat16),
            pltpu.VMEM((CORES * units, width), jnp.bfloat16),
            pltpu.VMEM((count, 2 * CORES * units), jnp.float32),
            pltpu.VMEM((count, CORES * units), jnp.float32),
            pltpu.SemaphoreType.DMA((8, steps)),
        ],
        compiler_params=pltpu.CompilerParams(vmem_limit_bytes=LIMIT),
        cost_estimate=cost(10 * count * width * CORES * units, 30 * MIB),
        name="middle",
    )(rows, *own, *sibling)


def grads_kernel(number, added, *refs):
    tokens, grads, hidden, deltas = (refs[i * number : (i + 1) * number] for i in range(4))
    gate, up, down = refs[-3:]
    units = gate.shape[1]
    both = sum(dot(t[...], d[...], FIRST_FIRST) for t, d in zip(tokens, deltas))
    low = sum(dot(h[...], g[...], FIRST_FIRST) for h, g in zip(hidden, grads))
    parts = [both[:, :units], both[:, units:], low]
    if added:
        received = refs[4 * number : 4 * number + 3]
        parts = [part + ref[...].astype(jnp.float32) for part, ref in zip(parts, received)]
    for ref, part in zip((gate, up, down), parts):
        ref[...] = part.astype(jnp.bfloat16)


def weight_grads(rows, hidden, deltas, core, received=()):
    counts = [part.shape[0] for part in rows]
    width = rows[0].shape[1] // 2
    units = hidden[0].shape[1] // CORES
    steps = 8
    span = width // steps
    tall = pl.BlockSpec((span, units), lambda i: (i, 0))
    wide = pl.BlockSpec((units, span), lambda i: (0, i))
    return pl.pallas_call(
        functools.partial(grads_kernel, len(rows), len(received) > 0),
        grid=(steps,),
        in_specs=[pl.BlockSpec((count, span), lambda i: (0, i)) for count in counts]
        + [pl.BlockSpec((count, span), lambda i: (0, i + steps)) for count in counts]
        + [pl.BlockSpec((count, units), lambda i: (0, core)) for count in counts]
        + [pl.BlockSpec((count, 2 * units), lambda i: (0, core)) for count in counts]
        + [tall, tall, wide][: len(received)],
        out_specs=[tall, tall, wide],
        out_shape=[
            jax.ShapeDtypeStruct((width, units), jnp.bfloat16),
            jax.ShapeDtypeStruct((width, units), jnp.bfloat16),
            jax.ShapeDtypeStruct((units, width), jnp.bfloat16),
        ],
        compiler_params=pltpu.CompilerParams(vmem_limit_bytes=LIMIT),
        cost_estimate=cost(6 * sum(counts) * width * units, 16 * MIB),
        name="own_grads" if received else "sibling_grads",
    )(*rows, *rows, *hidden, *deltas, *received)


def body(stash, out_grad, expert_ids, gate_probs, w_gate, w_up, w_down):
    chips = lax.axis_size("chip")
    sections = lax.axis_size("section")
    tokens = stash.shape[1]
    experts = chips * CORES // SPLIT
    capacity = tokens * 3 // (2 * experts)
    chunks = (2 * capacity // 3, capacity // 3)
    own = (w_gate[0, 0], w_up[0, 0], w_down[0, 0])
    sibling = tuple(swap_cores(weight) for weight in own)
    dealt, place_back = deal(
        expert_ids[0], gate_probs[0], stash[0], out_grad[0], experts, chunks
    )
    dealt, sibling = lax.optimization_barrier((dealt, sibling))
    rows = [over_chips(part) for part in dealt]
    hidden, deltas, returned = [], [], []
    back = None
    for part in rows:
        if back is not None:
            part, _ = lax.optimization_barrier((part, back))
        back, part_hidden, part_deltas = middle(part, own, sibling)
        returned.append(over_chips(back))
        hidden.append(part_hidden)
        deltas.append(part_deltas)
    input_grad = sum(dot(at, part) for at, part in zip(place_back, returned)).astype(jnp.bfloat16)
    prev_grad = lax.ppermute(
        input_grad, "section", [(i, (i - 1) % sections) for i in range(sections)]
    )
    theirs = weight_grads(rows, hidden, deltas, 1)
    received = tuple(swap_cores(part) for part in theirs)
    grads = weight_grads(rows, hidden, deltas, 0, received)
    return (prev_grad[None],) + tuple(grad[None, None] for grad in grads)


def solution(mesh):
    sections, devices = mesh.devices.shape
    fine = Mesh(mesh.devices.reshape(sections, devices // CORES, CORES), ("section", "chip", "core"))
    spec = P("section", ("chip", "core"))
    return jax.shard_map(
        body, mesh=fine, in_specs=(spec,) * 7, out_specs=(spec,) * 4, check_vma=False
    )
```

```python
import functools

import jax
import jax.numpy as jnp
from jax import lax
from jax.experimental import pallas as pl
from jax.experimental.pallas import tpu as pltpu
from jax.sharding import Mesh, PartitionSpec as P

SPLIT = 4
CORES = 2
HALVES = SPLIT // CORES
MIB = 1 << 20
LIMIT = 56 * MIB
NEXT_LAST = (((1,), (1,)), ((), ()))
FIRST_FIRST = (((0,), (0,)), ((), ()))


def dot(left, right, dims=(((1,), (0,)), ((), ()))):
    return lax.dot_general(left, right, dims, preferred_element_type=jnp.float32)


def swap_cores(value):
    return lax.ppermute(value, "core", [(0, 1), (1, 0)])


def over_chips(value):
    return lax.all_to_all(value, "chip", split_axis=0, concat_axis=0, tiled=True)


def cost(flops, moved):
    return pl.CostEstimate(flops=flops, bytes_accessed=moved, transcendentals=0)


def places(ids, rank, chunks, experts, slot_dim, shape):
    found = []
    at = 0
    for depth in chunks:
        slot = lax.broadcasted_iota(jnp.int32, shape(experts * HALVES * depth), slot_dim)
        inside = (rank >= at) & (rank < at + depth)
        first = ids * (HALVES * depth) + rank - at
        hit = (slot == first) | (slot == first + depth)
        found.append((hit & inside).astype(jnp.float32).astype(jnp.bfloat16))
        at += depth
    return found


def deal_kernel(experts, chunks, blocks, row_ids, col_ids, gates, stash, out_grad, *refs):
    number = len(chunks)
    dealt, place_back, place = refs[:number], refs[number : 2 * number], refs[2 * number :]
    step = pl.program_id(0)
    tokens = col_ids.shape[0]

    @pl.when(step == 0)
    def _():
        first = lax.broadcasted_iota(jnp.int32, (tokens, tokens), 0)
        second = lax.broadcasted_iota(jnp.int32, (tokens, tokens), 1)
        ids = row_ids[...]
        hot = (lax.broadcasted_iota(jnp.int32, (experts, tokens), 0) == ids).astype(jnp.float32)
        before = dot(hot.astype(jnp.bfloat16), (first < second).astype(jnp.bfloat16))
        rank = jnp.sum(before * hot, axis=0, keepdims=True).astype(jnp.int32)
        found = places(ids, rank, chunks, experts, 0, lambda slots: (slots, tokens))
        for ref, value in zip(place, found):
            ref[...] = value
        ids = col_ids[...]
        hot = (lax.broadcasted_iota(jnp.int32, (tokens, experts), 1) == ids).astype(jnp.float32)
        before = dot((second < first).astype(jnp.bfloat16), hot.astype(jnp.bfloat16))
        rank = jnp.sum(before * hot, axis=1, keepdims=True).astype(jnp.int32)
        found = places(ids, rank, chunks, experts, 1, lambda slots: (tokens, slots))
        for ref, value in zip(place_back, found):
            ref[...] = value

    @pl.when(step < blocks)
    def _():
        for ref, at in zip(dealt, place):
            ref[...] = dot(at[...], stash[...]).astype(jnp.bfloat16)

    @pl.when(step >= blocks)
    def _():
        scaled = (gates[...] * out_grad[...].astype(jnp.float32)).astype(jnp.bfloat16)
        for ref, at in zip(dealt, place):
            ref[...] = dot(at[...], scaled).astype(jnp.bfloat16)


def deal(ids, gates, stash, out_grad, experts, chunks):
    tokens, width = stash.shape
    slots = [experts * HALVES * depth for depth in chunks]
    blocks = 4
    span = width // blocks
    outs = pl.pallas_call(
        functools.partial(deal_kernel, experts, chunks, blocks),
        grid=(2 * blocks,),
        in_specs=[
            pl.BlockSpec((1, tokens), lambda i: (0, 0)),
            pl.BlockSpec((tokens, 1), lambda i: (0, 0)),
            pl.BlockSpec((tokens, 1), lambda i: (0, 0)),
            pl.BlockSpec((tokens, span), lambda i: (0, jnp.minimum(i, blocks - 1))),
            pl.BlockSpec((tokens, span), lambda i: (0, jnp.maximum(i - blocks, 0))),
        ],
        out_specs=[pl.BlockSpec((count, span), lambda i: (0, i)) for count in slots]
        + [pl.BlockSpec((tokens, count), lambda i: (0, 0)) for count in slots],
        out_shape=[jax.ShapeDtypeStruct((count, 2 * width), jnp.bfloat16) for count in slots]
        + [jax.ShapeDtypeStruct((tokens, count), jnp.bfloat16) for count in slots],
        scratch_shapes=[pltpu.VMEM((count, tokens), jnp.bfloat16) for count in slots],
        compiler_params=pltpu.CompilerParams(vmem_limit_bytes=16 * MIB),
        cost_estimate=cost(4 * sum(slots) * tokens * width, 6 * sum(slots) * width),
        name="deal_rows",
    )(ids.reshape(1, tokens), ids, gates, stash, out_grad)
    return outs[: len(chunks)], outs[len(chunks) :]


def middle_kernel(steps, cuts, rows_ref, go, uo, do, gs, us, ds, *refs):
    backs, refs = refs[: len(cuts)], refs[len(cuts) :]
    hidden, deltas, held, joined, down, pre, tail, out, sems, out_sems = refs
    rows, width = out.shape
    units = go.shape[1]
    span = width // steps

    def block(k, base=0):
        return pl.ds(pl.multiple_of(base + k * span, span), span)

    def copies(k):
        at, late = block(k), block(k, width)
        pairs = [
            (rows_ref.at[:, at], held.at[:, at]),
            (rows_ref.at[:, late], held.at[:, late]),
            (do.at[:, at], down.at[pl.ds(0, units), at]),
            (ds.at[:, at], down.at[pl.ds(units, units), at]),
        ]
        for i, weight in enumerate((go, uo, gs, us)):
            pairs.append((weight.at[at, :], joined.at[at, pl.ds(i * units, units)]))
        return [
            pltpu.make_async_copy(src, dst, sems.at[i, k]) for i, (src, dst) in enumerate(pairs)
        ]

    @pl.loop(0, steps)
    def _(k):
        for copy in copies(k):
            copy.start()

    pre[...] = jnp.zeros_like(pre)
    tail[...] = jnp.zeros_like(tail)

    @pl.loop(0, steps)
    def _(k):
        for copy in copies(k):
            copy.wait()
        at, late = block(k), block(k, width)
        pre[...] += dot(held[:, at], joined[at, :])
        tail[...] += dot(held[:, late], down[:, at], NEXT_LAST)

    @pl.loop(0, rows // 16)
    def _(r):
        at = pl.ds(pl.multiple_of(r * 16, 16), 16)
        for core in range(CORES):
            gate = slice(2 * core * units, (2 * core + 1) * units)
            up = slice((2 * core + 1) * units, (2 * core + 2) * units)
            own = slice(core * units, (core + 1) * units)
            gate_pre, up_pre, grad = pre[at, gate], pre[at, up], tail[at, own]
            sigmoid_a = jax.nn.sigmoid(gate_pre)
            silu_a = gate_pre * sigmoid_a
            hidden[at, own] = (silu_a * up_pre).astype(jnp.bfloat16)
            deltas[at, gate] = (
                grad * up_pre * sigmoid_a * (1.0 + gate_pre * (1.0 - sigmoid_a))
            ).astype(jnp.bfloat16)
            deltas[at, up] = (grad * silu_a).astype(jnp.bfloat16)

    def leave(back, k, begin):
        return pltpu.make_async_copy(out.at[:, block(k)], back.at[:, block(k - begin)], out_sems.at[k])

    begin = 0
    ranges = []
    for back, cut in zip(backs, cuts):
        ranges.append((back, begin, begin + cut // span))
        begin += cut // span
    for back, begin, end in ranges:

        @pl.loop(begin, end)
        def _(k):
            out[:, block(k)] = dot(deltas[...], joined[block(k), :], NEXT_LAST).astype(jnp.bfloat16)
            leave(back, k, begin).start()

    for back, begin, end in ranges:

        @pl.loop(begin, end)
        def _(k):
            leave(back, k, begin).wait()


def middle(rows, own, sibling, cuts):
    count, width = rows.shape[0], rows.shape[1] // 2
    units = own[0].shape[1]
    steps = 8
    anywhere = pl.BlockSpec(memory_space=pl.ANY)
    whole = pl.BlockSpec(memory_space=pltpu.VMEM)
    outs = pl.pallas_call(
        functools.partial(middle_kernel, steps, cuts),
        in_specs=[anywhere] * 7,
        out_specs=[anywhere] * len(cuts) + [whole] * 2,
        out_shape=[jax.ShapeDtypeStruct((count, cut), jnp.bfloat16) for cut in cuts]
        + [
            jax.ShapeDtypeStruct((count, CORES * units), jnp.bfloat16),
            jax.ShapeDtypeStruct((count, 2 * CORES * units), jnp.bfloat16),
        ],
        scratch_shapes=[
            pltpu.VMEM((count, 2 * width), jnp.bfloat16),
            pltpu.VMEM((width, 2 * CORES * units), jnp.bfloat16),
            pltpu.VMEM((CORES * units, width), jnp.bfloat16),
            pltpu.VMEM((count, 2 * CORES * units), jnp.float32),
            pltpu.VMEM((count, CORES * units), jnp.float32),
            pltpu.VMEM((count, width), jnp.bfloat16),
            pltpu.SemaphoreType.DMA((8, steps)),
            pltpu.SemaphoreType.DMA((steps,)),
        ],
        compiler_params=pltpu.CompilerParams(vmem_limit_bytes=40 * MIB),
        cost_estimate=cost(10 * count * width * CORES * units, 30 * MIB),
        name="middle",
    )(rows, *own, *sibling)
    return outs[: len(cuts)], outs[-2], outs[-1]


def grads_kernel(number, added, *refs):
    tokens, grads, hidden, deltas = (refs[i * number : (i + 1) * number] for i in range(4))
    gate, up, down = refs[-3:]
    units = gate.shape[1]
    both = sum(dot(t[...], d[...], FIRST_FIRST) for t, d in zip(tokens, deltas))
    low = sum(dot(h[...], g[...], FIRST_FIRST) for h, g in zip(hidden, grads))
    parts = [both[:, :units], both[:, units:], low]
    if added:
        received = refs[4 * number : 4 * number + 3]
        parts = [part + ref[...].astype(jnp.float32) for part, ref in zip(parts, received)]
    for ref, part in zip((gate, up, down), parts):
        ref[...] = part.astype(jnp.bfloat16)


def weight_grads(rows, hidden, deltas, core, received=()):
    counts = [part.shape[0] for part in rows]
    width = rows[0].shape[1] // 2
    units = hidden[0].shape[1] // CORES
    steps = 8
    span = width // steps
    tall = pl.BlockSpec((span, units), lambda i: (i, 0))
    wide = pl.BlockSpec((units, span), lambda i: (0, i))
    return pl.pallas_call(
        functools.partial(grads_kernel, len(rows), len(received) > 0),
        grid=(steps,),
        in_specs=[pl.BlockSpec((count, span), lambda i: (0, i)) for count in counts]
        + [pl.BlockSpec((count, span), lambda i: (0, i + steps)) for count in counts]
        + [pl.BlockSpec((count, units), lambda i: (0, core)) for count in counts]
        + [pl.BlockSpec((count, 2 * units), lambda i: (0, core)) for count in counts]
        + [tall, tall, wide][: len(received)],
        out_specs=[tall, tall, wide],
        out_shape=[
            jax.ShapeDtypeStruct((width, units), jnp.bfloat16),
            jax.ShapeDtypeStruct((width, units), jnp.bfloat16),
            jax.ShapeDtypeStruct((units, width), jnp.bfloat16),
        ],
        compiler_params=pltpu.CompilerParams(vmem_limit_bytes=LIMIT),
        cost_estimate=cost(6 * sum(counts) * width * units, 16 * MIB),
        name="own_grads" if received else "sibling_grads",
    )(*rows, *rows, *hidden, *deltas, *received)


def body(stash, out_grad, expert_ids, gate_probs, w_gate, w_up, w_down):
    chips = lax.axis_size("chip")
    sections = lax.axis_size("section")
    tokens = stash.shape[1]
    experts = chips * CORES // SPLIT
    capacity = tokens * 3 // (2 * experts)
    own = (w_gate[0, 0], w_up[0, 0], w_down[0, 0])
    sibling = tuple(swap_cores(weight) for weight in own)
    (dealt,), (place_back,) = deal(
        expert_ids[0], gate_probs[0], stash[0], out_grad[0], experts, (capacity,)
    )
    dealt, sibling = lax.optimization_barrier((dealt, sibling))
    rows = over_chips(dealt)
    width = stash.shape[2]
    backs, hidden, deltas = middle(rows, own, sibling, (width * 3 // 4, width // 4))
    theirs = weight_grads([rows], [hidden], [deltas], 1)
    received = tuple(swap_cores(part) for part in theirs)

    def shift(returned):
        input_grad = dot(place_back, returned).astype(jnp.bfloat16)
        return input_grad, lambda value: lax.ppermute(
            value, "section", [(i, (i - 1) % sections) for i in range(sections)]
        )

    first = over_chips(backs[0])
    last, first = lax.optimization_barrier((backs[1], first))
    last = over_chips(last)
    first, move = shift(first)
    deltas, first = lax.optimization_barrier((deltas, first))
    first = move(first)
    grads = weight_grads([rows], [hidden], [deltas], 0, received)
    last, move = shift(last)
    last, grads = lax.optimization_barrier((last, tuple(grads)))
    last = move(last)
    prev_grad = jnp.concatenate([first, last], axis=1)
    return (prev_grad[None],) + tuple(grad[None, None] for grad in grads)


def solution(mesh):
    sections, devices = mesh.devices.shape
    fine = Mesh(mesh.devices.reshape(sections, devices // CORES, CORES), ("section", "chip", "core"))
    spec = P("section", ("chip", "core"))
    return jax.shard_map(
        body, mesh=fine, in_specs=(spec,) * 7, out_specs=(spec,) * 4, check_vma=False
    )
```

```python
import functools

import jax
import jax.numpy as jnp
from jax import lax
from jax.experimental import pallas as pl
from jax.experimental.pallas import tpu as pltpu
from jax.sharding import Mesh, PartitionSpec as P

SPLIT = 4
CORES = 2
HALVES = SPLIT // CORES
MIB = 1 << 20
LIMIT = 56 * MIB
NEXT_LAST = (((1,), (1,)), ((), ()))
FIRST_FIRST = (((0,), (0,)), ((), ()))


def dot(left, right, dims=(((1,), (0,)), ((), ()))):
    return lax.dot_general(left, right, dims, preferred_element_type=jnp.float32)


def swap_cores(value):
    return lax.ppermute(value, "core", [(0, 1), (1, 0)])


def over_chips(value):
    return lax.all_to_all(value, "chip", split_axis=0, concat_axis=0, tiled=True)


def cost(flops, moved):
    return pl.CostEstimate(flops=flops, bytes_accessed=moved, transcendentals=0)


def places(ids, rank, chunks, experts, slot_dim, shape):
    found = []
    at = 0
    for depth in chunks:
        slot = lax.broadcasted_iota(jnp.int32, shape(experts * HALVES * depth), slot_dim)
        inside = (rank >= at) & (rank < at + depth)
        first = ids * (HALVES * depth) + rank - at
        hit = (slot == first) | (slot == first + depth)
        found.append((hit & inside).astype(jnp.float32).astype(jnp.bfloat16))
        at += depth
    return found


def deal_kernel(experts, chunks, blocks, row_ids, col_ids, gates, stash, out_grad, *refs):
    number = len(chunks)
    dealt, place_back, place = refs[:number], refs[number : 2 * number], refs[2 * number :]
    step = pl.program_id(0)
    tokens = col_ids.shape[0]

    @pl.when(step == 0)
    def _():
        first = lax.broadcasted_iota(jnp.int32, (tokens, tokens), 0)
        second = lax.broadcasted_iota(jnp.int32, (tokens, tokens), 1)
        ids = row_ids[...]
        hot = (lax.broadcasted_iota(jnp.int32, (experts, tokens), 0) == ids).astype(jnp.float32)
        before = dot(hot.astype(jnp.bfloat16), (first < second).astype(jnp.bfloat16))
        rank = jnp.sum(before * hot, axis=0, keepdims=True).astype(jnp.int32)
        found = places(ids, rank, chunks, experts, 0, lambda slots: (slots, tokens))
        for ref, value in zip(place, found):
            ref[...] = value
        ids = col_ids[...]
        hot = (lax.broadcasted_iota(jnp.int32, (tokens, experts), 1) == ids).astype(jnp.float32)
        before = dot((second < first).astype(jnp.bfloat16), hot.astype(jnp.bfloat16))
        rank = jnp.sum(before * hot, axis=1, keepdims=True).astype(jnp.int32)
        found = places(ids, rank, chunks, experts, 1, lambda slots: (tokens, slots))
        for ref, value in zip(place_back, found):
            ref[...] = value

    @pl.when(step < blocks)
    def _():
        for ref, at in zip(dealt, place):
            ref[...] = dot(at[...], stash[...]).astype(jnp.bfloat16)

    @pl.when(step >= blocks)
    def _():
        scaled = (gates[...] * out_grad[...].astype(jnp.float32)).astype(jnp.bfloat16)
        for ref, at in zip(dealt, place):
            ref[...] = dot(at[...], scaled).astype(jnp.bfloat16)


def deal(ids, gates, stash, out_grad, experts, chunks):
    tokens, width = stash.shape
    slots = [experts * HALVES * depth for depth in chunks]
    blocks = 4
    span = width // blocks
    outs = pl.pallas_call(
        functools.partial(deal_kernel, experts, chunks, blocks),
        grid=(2 * blocks,),
        in_specs=[
            pl.BlockSpec((1, tokens), lambda i: (0, 0)),
            pl.BlockSpec((tokens, 1), lambda i: (0, 0)),
            pl.BlockSpec((tokens, 1), lambda i: (0, 0)),
            pl.BlockSpec((tokens, span), lambda i: (0, jnp.minimum(i, blocks - 1))),
            pl.BlockSpec((tokens, span), lambda i: (0, jnp.maximum(i - blocks, 0))),
        ],
        out_specs=[pl.BlockSpec((count, span), lambda i: (0, i)) for count in slots]
        + [pl.BlockSpec((tokens, count), lambda i: (0, 0)) for count in slots],
        out_shape=[jax.ShapeDtypeStruct((count, 2 * width), jnp.bfloat16) for count in slots]
        + [jax.ShapeDtypeStruct((tokens, count), jnp.bfloat16) for count in slots],
        scratch_shapes=[pltpu.VMEM((count, tokens), jnp.bfloat16) for count in slots],
        compiler_params=pltpu.CompilerParams(vmem_limit_bytes=LIMIT),
        cost_estimate=cost(4 * sum(slots) * tokens * width, 6 * sum(slots) * width),
        name="deal_rows",
    )(ids.reshape(1, tokens), ids, gates, stash, out_grad)
    return outs[: len(chunks)], outs[len(chunks) :]


def middle_kernel(steps, rows_ref, go, uo, do, gs, us, ds, back, *refs):
    hidden, deltas, held, joined, down, pre, tail, out, sems, out_sems = refs
    rows, width = held.shape[0], held.shape[1] // 2
    units = go.shape[1]
    span = width // steps

    def block(k, base=0):
        return pl.ds(pl.multiple_of(base + k * span, span), span)

    def copies(k):
        at, late = block(k), block(k, width)
        pairs = [
            (rows_ref.at[:, at], held.at[:, at]),
            (rows_ref.at[:, late], held.at[:, late]),
            (do.at[:, at], down.at[pl.ds(0, units), at]),
            (ds.at[:, at], down.at[pl.ds(units, units), at]),
        ]
        for i, weight in enumerate((go, uo, gs, us)):
            pairs.append((weight.at[at, :], joined.at[at, pl.ds(i * units, units)]))
        return [
            pltpu.make_async_copy(src, dst, sems.at[i, k]) for i, (src, dst) in enumerate(pairs)
        ]

    @pl.loop(0, steps)
    def _(k):
        for copy in copies(k):
            copy.start()

    pre[...] = jnp.zeros_like(pre)
    tail[...] = jnp.zeros_like(tail)

    @pl.loop(0, steps)
    def _(k):
        for copy in copies(k):
            copy.wait()
        at, late = block(k), block(k, width)
        pre[...] += dot(held[:, at], joined[at, :])
        tail[...] += dot(held[:, late], down[:, at], NEXT_LAST)

    @pl.loop(0, rows // 16)
    def _(r):
        at = pl.ds(pl.multiple_of(r * 16, 16), 16)
        for core in range(CORES):
            gate = slice(2 * core * units, (2 * core + 1) * units)
            up = slice((2 * core + 1) * units, (2 * core + 2) * units)
            own = slice(core * units, (core + 1) * units)
            gate_pre, up_pre, grad = pre[at, gate], pre[at, up], tail[at, own]
            sigmoid_a = jax.nn.sigmoid(gate_pre)
            silu_a = gate_pre * sigmoid_a
            hidden[at, own] = (silu_a * up_pre).astype(jnp.bfloat16)
            deltas[at, gate] = (
                grad * up_pre * sigmoid_a * (1.0 + gate_pre * (1.0 - sigmoid_a))
            ).astype(jnp.bfloat16)
            deltas[at, up] = (grad * silu_a).astype(jnp.bfloat16)

    def leave(k):
        return pltpu.make_async_copy(out.at[:, block(k)], back.at[:, block(k)], out_sems.at[k])

    @pl.loop(0, back.shape[1] // span)
    def _(k):
        out[:, block(k)] = dot(deltas[...], joined[block(k), :], NEXT_LAST).astype(jnp.bfloat16)
        leave(k).start()

    @pl.loop(0, back.shape[1] // span)
    def _(k):
        leave(k).wait()


def middle(rows, own, sibling, cut):
    count, width = rows.shape[0], rows.shape[1] // 2
    units = own[0].shape[1]
    steps = 8
    anywhere = pl.BlockSpec(memory_space=pl.ANY)
    whole = pl.BlockSpec(memory_space=pltpu.VMEM)
    return pl.pallas_call(
        functools.partial(middle_kernel, steps),
        in_specs=[anywhere] * 7,
        out_specs=[anywhere] + [whole] * 2,
        out_shape=[
            jax.ShapeDtypeStruct((count, cut), jnp.bfloat16),
            jax.ShapeDtypeStruct((count, CORES * units), jnp.bfloat16),
            jax.ShapeDtypeStruct((count, 2 * CORES * units), jnp.bfloat16),
        ],
        scratch_shapes=[
            pltpu.VMEM((count, 2 * width), jnp.bfloat16),
            pltpu.VMEM((width, 2 * CORES * units), jnp.bfloat16),
            pltpu.VMEM((CORES * units, width), jnp.bfloat16),
            pltpu.VMEM((count, 2 * CORES * units), jnp.float32),
            pltpu.VMEM((count, CORES * units), jnp.float32),
            pltpu.VMEM((count, cut), jnp.bfloat16),
            pltpu.SemaphoreType.DMA((8, steps)),
            pltpu.SemaphoreType.DMA((steps,)),
        ],
        compiler_params=pltpu.CompilerParams(vmem_limit_bytes=LIMIT),
        cost_estimate=cost(8 * count * width * CORES * units, 30 * MIB),
        name="middle",
    )(rows, *own, *sibling)


def rest_kernel(deltas, *refs):
    weights, back = refs[:-1], refs[-1]
    units = weights[0].shape[1]
    total = dot(deltas[:, :units], weights[0][...], NEXT_LAST)
    for i, weight in enumerate(weights[1:], 1):
        total += dot(deltas[:, i * units : (i + 1) * units], weight[...], NEXT_LAST)
    back[...] = total.astype(jnp.bfloat16)


def rest(deltas, own, sibling, cut):
    count = deltas.shape[0]
    width, units = own[0].shape
    span = width // 8
    first = cut // span
    return pl.pallas_call(
        rest_kernel,
        grid=(width // span - first,),
        in_specs=[pl.BlockSpec(deltas.shape, lambda i: (0, 0))]
        + [pl.BlockSpec((span, units), lambda i: (i + first, 0))] * 4,
        out_specs=pl.BlockSpec((count, span), lambda i: (0, i)),
        out_shape=jax.ShapeDtypeStruct((count, width - cut), jnp.bfloat16),
        compiler_params=pltpu.CompilerParams(vmem_limit_bytes=LIMIT),
        cost_estimate=cost(8 * count * (width - cut) * units, 8 * MIB),
        name="last_columns",
    )(deltas, *own[:2], *sibling[:2])


def combine_kernel(place_back, returned, mark, out):
    out[...] = dot(place_back[...], returned[...]).astype(jnp.bfloat16)


def combine(place_back, returned, mark):
    tokens, slots = place_back.shape
    width = returned.shape[1]
    span = width // 3
    return pl.pallas_call(
        combine_kernel,
        grid=(width // span,),
        in_specs=[
            pl.BlockSpec((tokens, slots), lambda i: (0, 0)),
            pl.BlockSpec((slots, span), lambda i: (0, i)),
            pl.BlockSpec(memory_space=pl.ANY),
        ],
        out_specs=pl.BlockSpec((tokens, span), lambda i: (0, i)),
        out_shape=jax.ShapeDtypeStruct((tokens, width), jnp.bfloat16),
        compiler_params=pltpu.CompilerParams(vmem_limit_bytes=LIMIT),
        cost_estimate=cost(2 * tokens * slots * width, 2 * slots * width),
        name="combine",
    )(place_back, returned, mark)


def grads_kernel(number, added, *refs):
    tokens, grads, hidden, deltas = (refs[i * number : (i + 1) * number] for i in range(4))
    gate, up, down = refs[-3:]
    units = gate.shape[1]
    both = sum(dot(t[...], d[...], FIRST_FIRST) for t, d in zip(tokens, deltas))
    low = sum(dot(h[...], g[...], FIRST_FIRST) for h, g in zip(hidden, grads))
    parts = [both[:, :units], both[:, units:], low]
    if added:
        received = refs[4 * number : 4 * number + 3]
        parts = [part + ref[...].astype(jnp.float32) for part, ref in zip(parts, received)]
    for ref, part in zip((gate, up, down), parts):
        ref[...] = part.astype(jnp.bfloat16)


def weight_grads(rows, hidden, deltas, core, received=()):
    counts = [part.shape[0] for part in rows]
    width = rows[0].shape[1] // 2
    units = hidden[0].shape[1] // CORES
    steps = 8
    span = width // steps
    tall = pl.BlockSpec((span, units), lambda i: (i, 0))
    wide = pl.BlockSpec((units, span), lambda i: (0, i))
    return pl.pallas_call(
        functools.partial(grads_kernel, len(rows), len(received) > 0),
        grid=(steps,),
        in_specs=[pl.BlockSpec((count, span), lambda i: (0, i)) for count in counts]
        + [pl.BlockSpec((count, span), lambda i: (0, i + steps)) for count in counts]
        + [pl.BlockSpec((count, units), lambda i: (0, core)) for count in counts]
        + [pl.BlockSpec((count, 2 * units), lambda i: (0, core)) for count in counts]
        + [tall, tall, wide][: len(received)],
        out_specs=[tall, tall, wide],
        out_shape=[
            jax.ShapeDtypeStruct((width, units), jnp.bfloat16),
            jax.ShapeDtypeStruct((width, units), jnp.bfloat16),
            jax.ShapeDtypeStruct((units, width), jnp.bfloat16),
        ],
        compiler_params=pltpu.CompilerParams(vmem_limit_bytes=LIMIT),
        cost_estimate=cost(6 * sum(counts) * width * units, 16 * MIB),
        name="own_grads" if received else "sibling_grads",
    )(*rows, *rows, *hidden, *deltas, *received)


def body(stash, out_grad, expert_ids, gate_probs, w_gate, w_up, w_down):
    chips = lax.axis_size("chip")
    sections = lax.axis_size("section")
    tokens = stash.shape[1]
    experts = chips * CORES // SPLIT
    capacity = tokens * 3 // (2 * experts)
    own = (w_gate[0, 0], w_up[0, 0], w_down[0, 0])
    sibling = tuple(swap_cores(weight) for weight in own)
    (dealt,), (place_back,) = deal(
        expert_ids[0], gate_probs[0], stash[0], out_grad[0], experts, (capacity,)
    )
    dealt, sibling = lax.optimization_barrier((dealt, sibling))
    rows = over_chips(dealt)
    width = stash.shape[2]
    cut = width * 5 // 8
    back, hidden, deltas = middle(rows, own, sibling, cut)
    last = rest(deltas, own, sibling, cut)
    theirs = weight_grads([rows], [hidden], [deltas], 1)
    received = tuple(swap_cores(part) for part in theirs)

    def shift(value):
        return lax.ppermute(value, "section", [(i, (i - 1) % sections) for i in range(sections)])

    first = over_chips(back)
    last, first = lax.optimization_barrier((last, first))
    last = over_chips(last)
    first = dot(place_back, first).astype(jnp.bfloat16)
    deltas, first = lax.optimization_barrier((deltas, first))
    first = shift(first)
    grads = weight_grads([rows], [hidden], [deltas], 0, received)
    mark = swap_cores(grads[0][:16, :128])
    last = shift(combine(place_back, last, mark))
    prev_grad = jnp.concatenate([first, last], axis=1)
    return (prev_grad[None],) + tuple(grad[None, None] for grad in grads)


def solution(mesh):
    sections, devices = mesh.devices.shape
    fine = Mesh(mesh.devices.reshape(sections, devices // CORES, CORES), ("section", "chip", "core"))
    spec = P("section", ("chip", "core"))
    return jax.shard_map(
        body, mesh=fine, in_specs=(spec,) * 7, out_specs=(spec,) * 4, check_vma=False
    )
```

```python
import functools

import jax
import jax.numpy as jnp
from jax import lax
from jax.experimental import pallas as pl
from jax.experimental.pallas import tpu as pltpu
from jax.sharding import Mesh, PartitionSpec as P

SPLIT = 4
CORES = 2
HALVES = SPLIT // CORES
MIB = 1 << 20
LIMIT = 56 * MIB
NEXT_LAST = (((1,), (1,)), ((), ()))
FIRST_FIRST = (((0,), (0,)), ((), ()))


def dot(left, right, dims=(((1,), (0,)), ((), ()))):
    return lax.dot_general(left, right, dims, preferred_element_type=jnp.float32)


def swap_cores(value):
    return lax.ppermute(value, "core", [(0, 1), (1, 0)])


def over_chips(value):
    return lax.all_to_all(value, "chip", split_axis=0, concat_axis=0, tiled=True)


def cost(flops, moved):
    return pl.CostEstimate(flops=flops, bytes_accessed=moved, transcendentals=0)


def places(ids, rank, chunks, experts, slot_dim, shape):
    found = []
    at = 0
    for depth in chunks:
        slot = lax.broadcasted_iota(jnp.int32, shape(experts * HALVES * depth), slot_dim)
        inside = (rank >= at) & (rank < at + depth)
        first = ids * (HALVES * depth) + rank - at
        hit = (slot == first) | (slot == first + depth)
        found.append((hit & inside).astype(jnp.float32).astype(jnp.bfloat16))
        at += depth
    return found


def deal_kernel(experts, chunks, blocks, row_ids, col_ids, gates, stash, out_grad, *refs):
    number = len(chunks)
    dealt, place_back, place = refs[:number], refs[number : 2 * number], refs[2 * number :]
    step = pl.program_id(0)
    tokens = col_ids.shape[0]

    @pl.when(step == 0)
    def _():
        first = lax.broadcasted_iota(jnp.int32, (tokens, tokens), 0)
        second = lax.broadcasted_iota(jnp.int32, (tokens, tokens), 1)
        ids = row_ids[...]
        hot = (lax.broadcasted_iota(jnp.int32, (experts, tokens), 0) == ids).astype(jnp.float32)
        before = dot(hot.astype(jnp.bfloat16), (first < second).astype(jnp.bfloat16))
        rank = jnp.sum(before * hot, axis=0, keepdims=True).astype(jnp.int32)
        found = places(ids, rank, chunks, experts, 0, lambda slots: (slots, tokens))
        for ref, value in zip(place, found):
            ref[...] = value
        ids = col_ids[...]
        hot = (lax.broadcasted_iota(jnp.int32, (tokens, experts), 1) == ids).astype(jnp.float32)
        before = dot((second < first).astype(jnp.bfloat16), hot.astype(jnp.bfloat16))
        rank = jnp.sum(before * hot, axis=1, keepdims=True).astype(jnp.int32)
        found = places(ids, rank, chunks, experts, 1, lambda slots: (tokens, slots))
        for ref, value in zip(place_back, found):
            ref[...] = value

    @pl.when(step < blocks)
    def _():
        for ref, at in zip(dealt, place):
            ref[...] = dot(at[...], stash[...]).astype(jnp.bfloat16)

    @pl.when(step >= blocks)
    def _():
        scaled = (gates[...] * out_grad[...].astype(jnp.float32)).astype(jnp.bfloat16)
        for ref, at in zip(dealt, place):
            ref[...] = dot(at[...], scaled).astype(jnp.bfloat16)


def deal(ids, gates, stash, out_grad, experts, chunks):
    tokens, width = stash.shape
    slots = [experts * HALVES * depth for depth in chunks]
    blocks = 4
    span = width // blocks
    outs = pl.pallas_call(
        functools.partial(deal_kernel, experts, chunks, blocks),
        grid=(2 * blocks,),
        in_specs=[
            pl.BlockSpec((1, tokens), lambda i: (0, 0)),
            pl.BlockSpec((tokens, 1), lambda i: (0, 0)),
            pl.BlockSpec((tokens, 1), lambda i: (0, 0)),
            pl.BlockSpec((tokens, span), lambda i: (0, jnp.minimum(i, blocks - 1))),
            pl.BlockSpec((tokens, span), lambda i: (0, jnp.maximum(i - blocks, 0))),
        ],
        out_specs=[pl.BlockSpec((count, span), lambda i: (0, i)) for count in slots]
        + [pl.BlockSpec((tokens, count), lambda i: (0, 0)) for count in slots],
        out_shape=[jax.ShapeDtypeStruct((count, 2 * width), jnp.bfloat16) for count in slots]
        + [jax.ShapeDtypeStruct((tokens, count), jnp.bfloat16) for count in slots],
        scratch_shapes=[pltpu.VMEM((count, tokens), jnp.bfloat16) for count in slots],
        compiler_params=pltpu.CompilerParams(vmem_limit_bytes=16 * MIB),
        cost_estimate=cost(4 * sum(slots) * tokens * width, 6 * sum(slots) * width),
        name="deal_rows",
    )(ids.reshape(1, tokens), ids, gates, stash, out_grad)
    return outs[: len(chunks)], outs[len(chunks) :]


def middle_kernel(steps, cuts, rows_ref, go, uo, do, gs, us, ds, *refs):
    backs, refs = refs[: len(cuts)], refs[len(cuts) :]
    hidden, deltas, held, joined, down, pre, tail, out, sems, out_sems = refs
    rows, width = out.shape
    units = go.shape[1]
    span = width // steps

    def block(k, base=0):
        return pl.ds(pl.multiple_of(base + k * span, span), span)

    def copies(k):
        at, late = block(k), block(k, width)
        pairs = [
            (rows_ref.at[:, at], held.at[:, at]),
            (rows_ref.at[:, late], held.at[:, late]),
            (do.at[:, at], down.at[pl.ds(0, units), at]),
            (ds.at[:, at], down.at[pl.ds(units, units), at]),
        ]
        for i, weight in enumerate((go, uo, gs, us)):
            pairs.append((weight.at[at, :], joined.at[at, pl.ds(i * units, units)]))
        return [
            pltpu.make_async_copy(src, dst, sems.at[i, k]) for i, (src, dst) in enumerate(pairs)
        ]

    @pl.loop(0, steps)
    def _(k):
        for copy in copies(k):
            copy.start()

    pre[...] = jnp.zeros_like(pre)
    tail[...] = jnp.zeros_like(tail)

    @pl.loop(0, steps)
    def _(k):
        for copy in copies(k):
            copy.wait()
        at, late = block(k), block(k, width)
        pre[...] += dot(held[:, at], joined[at, :])
        tail[...] += dot(held[:, late], down[:, at], NEXT_LAST)

    @pl.loop(0, rows // 16)
    def _(r):
        at = pl.ds(pl.multiple_of(r * 16, 16), 16)
        for core in range(CORES):
            gate = slice(2 * core * units, (2 * core + 1) * units)
            up = slice((2 * core + 1) * units, (2 * core + 2) * units)
            own = slice(core * units, (core + 1) * units)
            gate_pre, up_pre, grad = pre[at, gate], pre[at, up], tail[at, own]
            sigmoid_a = jax.nn.sigmoid(gate_pre)
            silu_a = gate_pre * sigmoid_a
            hidden[at, own] = (silu_a * up_pre).astype(jnp.bfloat16)
            deltas[at, gate] = (
                grad * up_pre * sigmoid_a * (1.0 + gate_pre * (1.0 - sigmoid_a))
            ).astype(jnp.bfloat16)
            deltas[at, up] = (grad * silu_a).astype(jnp.bfloat16)

    def leave(back, k, begin):
        return pltpu.make_async_copy(out.at[:, block(k)], back.at[:, block(k - begin)], out_sems.at[k])

    begin = 0
    ranges = []
    for back, cut in zip(backs, cuts):
        ranges.append((back, begin, begin + cut // span))
        begin += cut // span
    for back, begin, end in ranges:

        @pl.loop(begin, end)
        def _(k):
            out[:, block(k)] = dot(deltas[...], joined[block(k), :], NEXT_LAST).astype(jnp.bfloat16)
            leave(back, k, begin).start()

    for back, begin, end in ranges:

        @pl.loop(begin, end)
        def _(k):
            leave(back, k, begin).wait()


def middle(rows, own, sibling, cuts):
    count, width = rows.shape[0], rows.shape[1] // 2
    units = own[0].shape[1]
    steps = 8
    anywhere = pl.BlockSpec(memory_space=pl.ANY)
    whole = pl.BlockSpec(memory_space=pltpu.VMEM)
    outs = pl.pallas_call(
        functools.partial(middle_kernel, steps, cuts),
        in_specs=[anywhere] * 7,
        out_specs=[anywhere] * len(cuts) + [whole] * 2,
        out_shape=[jax.ShapeDtypeStruct((count, cut), jnp.bfloat16) for cut in cuts]
        + [
            jax.ShapeDtypeStruct((count, CORES * units), jnp.bfloat16),
            jax.ShapeDtypeStruct((count, 2 * CORES * units), jnp.bfloat16),
        ],
        scratch_shapes=[
            pltpu.VMEM((count, 2 * width), jnp.bfloat16),
            pltpu.VMEM((width, 2 * CORES * units), jnp.bfloat16),
            pltpu.VMEM((CORES * units, width), jnp.bfloat16),
            pltpu.VMEM((count, 2 * CORES * units), jnp.float32),
            pltpu.VMEM((count, CORES * units), jnp.float32),
            pltpu.VMEM((count, width), jnp.bfloat16),
            pltpu.SemaphoreType.DMA((8, steps)),
            pltpu.SemaphoreType.DMA((steps,)),
        ],
        compiler_params=pltpu.CompilerParams(vmem_limit_bytes=LIMIT),
        cost_estimate=cost(10 * count * width * CORES * units, 30 * MIB),
        name="middle",
    )(rows, *own, *sibling)
    return outs[: len(cuts)], outs[-2], outs[-1]


def combine_kernel(place_back, returned, mark, out):
    out[...] = dot(place_back[...], returned[...]).astype(jnp.bfloat16)


def combine(place_back, returned, mark):
    tokens, slots = place_back.shape
    width = returned.shape[1]
    span = width // 3
    return pl.pallas_call(
        combine_kernel,
        grid=(width // span,),
        in_specs=[
            pl.BlockSpec((tokens, slots), lambda i: (0, 0)),
            pl.BlockSpec((slots, span), lambda i: (0, i)),
            pl.BlockSpec(memory_space=pl.ANY),
        ],
        out_specs=pl.BlockSpec((tokens, span), lambda i: (0, i)),
        out_shape=jax.ShapeDtypeStruct((tokens, width), jnp.bfloat16),
        compiler_params=pltpu.CompilerParams(vmem_limit_bytes=LIMIT),
        cost_estimate=cost(2 * tokens * slots * width, 2 * slots * width),
        name="combine",
    )(place_back, returned, mark)


def grads_kernel(number, added, *refs):
    tokens, grads, hidden, deltas = (refs[i * number : (i + 1) * number] for i in range(4))
    gate, up, down = refs[-3:]
    units = gate.shape[1]
    both = sum(dot(t[...], d[...], FIRST_FIRST) for t, d in zip(tokens, deltas))
    low = sum(dot(h[...], g[...], FIRST_FIRST) for h, g in zip(hidden, grads))
    parts = [both[:, :units], both[:, units:], low]
    if added:
        received = refs[4 * number : 4 * number + 3]
        parts = [part + ref[...].astype(jnp.float32) for part, ref in zip(parts, received)]
    for ref, part in zip((gate, up, down), parts):
        ref[...] = part.astype(jnp.bfloat16)


def weight_grads(rows, hidden, deltas, core, received=()):
    counts = [part.shape[0] for part in rows]
    width = rows[0].shape[1] // 2
    units = hidden[0].shape[1] // CORES
    steps = 8
    span = width // steps
    tall = pl.BlockSpec((span, units), lambda i: (i, 0))
    wide = pl.BlockSpec((units, span), lambda i: (0, i))
    return pl.pallas_call(
        functools.partial(grads_kernel, len(rows), len(received) > 0),
        grid=(steps,),
        in_specs=[pl.BlockSpec((count, span), lambda i: (0, i)) for count in counts]
        + [pl.BlockSpec((count, span), lambda i: (0, i + steps)) for count in counts]
        + [pl.BlockSpec((count, units), lambda i: (0, core)) for count in counts]
        + [pl.BlockSpec((count, 2 * units), lambda i: (0, core)) for count in counts]
        + [tall, tall, wide][: len(received)],
        out_specs=[tall, tall, wide],
        out_shape=[
            jax.ShapeDtypeStruct((width, units), jnp.bfloat16),
            jax.ShapeDtypeStruct((width, units), jnp.bfloat16),
            jax.ShapeDtypeStruct((units, width), jnp.bfloat16),
        ],
        compiler_params=pltpu.CompilerParams(vmem_limit_bytes=LIMIT),
        cost_estimate=cost(6 * sum(counts) * width * units, 16 * MIB),
        name="own_grads" if received else "sibling_grads",
    )(*rows, *rows, *hidden, *deltas, *received)


def body(stash, out_grad, expert_ids, gate_probs, w_gate, w_up, w_down):
    chips = lax.axis_size("chip")
    sections = lax.axis_size("section")
    tokens = stash.shape[1]
    experts = chips * CORES // SPLIT
    capacity = tokens * 3 // (2 * experts)
    own = (w_gate[0, 0], w_up[0, 0], w_down[0, 0])
    sibling = tuple(swap_cores(weight) for weight in own)
    (dealt,), (place_back,) = deal(
        expert_ids[0], gate_probs[0], stash[0], out_grad[0], experts, (capacity,)
    )
    dealt, sibling = lax.optimization_barrier((dealt, sibling))
    rows = over_chips(dealt)
    width = stash.shape[2]
    cut = width * 5 // 8
    backs, hidden, deltas = middle(rows, own, sibling, (cut, width - cut))
    theirs = weight_grads([rows], [hidden], [deltas], 1)
    received = tuple(swap_cores(part) for part in theirs)

    def shift(value):
        return lax.ppermute(value, "section", [(i, (i - 1) % sections) for i in range(sections)])

    first = over_chips(backs[0])
    last, first = lax.optimization_barrier((backs[1], first))
    last = over_chips(last)
    first = dot(place_back, first).astype(jnp.bfloat16)
    deltas, first = lax.optimization_barrier((deltas, first))
    first = shift(first)
    grads = weight_grads([rows], [hidden], [deltas], 0, received)
    mark = swap_cores(grads[0][:16, :128])
    last = shift(combine(place_back, last, mark))
    prev_grad = jnp.concatenate([first, last], axis=1)
    return (prev_grad[None],) + tuple(grad[None, None] for grad in grads)


def solution(mesh):
    sections, devices = mesh.devices.shape
    fine = Mesh(mesh.devices.reshape(sections, devices // CORES, CORES), ("section", "chip", "core"))
    spec = P("section", ("chip", "core"))
    return jax.shard_map(
        body, mesh=fine, in_specs=(spec,) * 7, out_specs=(spec,) * 4, check_vma=False
    )
```

```python
import functools

import jax
import jax.numpy as jnp
from jax import lax
from jax.experimental import pallas as pl
from jax.experimental.pallas import tpu as pltpu
from jax.sharding import Mesh, PartitionSpec as P

SPLIT = 4
CORES = 2
HALVES = SPLIT // CORES
MIB = 1 << 20
LIMIT = 32 * MIB
NEXT_LAST = (((1,), (1,)), ((), ()))
FIRST_FIRST = (((0,), (0,)), ((), ()))


def dot(left, right, dims=(((1,), (0,)), ((), ()))):
    return lax.dot_general(left, right, dims, preferred_element_type=jnp.float32)


def swap_cores(value):
    return lax.ppermute(value, "core", [(0, 1), (1, 0)])


def over_chips(value):
    return lax.all_to_all(value, "chip", split_axis=0, concat_axis=0, tiled=True)


def cost(flops, moved):
    return pl.CostEstimate(flops=flops, bytes_accessed=moved, transcendentals=0)


def places(ids, rank, chunks, experts, slot_dim, shape):
    found = []
    at = 0
    for depth in chunks:
        slot = lax.broadcasted_iota(jnp.int32, shape(experts * HALVES * depth), slot_dim)
        inside = (rank >= at) & (rank < at + depth)
        first = ids * (HALVES * depth) + rank - at
        hit = (slot == first) | (slot == first + depth)
        found.append((hit & inside).astype(jnp.float32).astype(jnp.bfloat16))
        at += depth
    return found


def deal_kernel(experts, chunks, blocks, row_ids, col_ids, gates, stash, out_grad, *refs):
    number = len(chunks)
    dealt, place_back, place = refs[:number], refs[number : 2 * number], refs[2 * number :]
    step = pl.program_id(0)
    tokens = col_ids.shape[0]

    @pl.when(step == 0)
    def _():
        first = lax.broadcasted_iota(jnp.int32, (tokens, tokens), 0)
        second = lax.broadcasted_iota(jnp.int32, (tokens, tokens), 1)
        ids = row_ids[...]
        hot = (lax.broadcasted_iota(jnp.int32, (experts, tokens), 0) == ids).astype(jnp.float32)
        before = dot(hot.astype(jnp.bfloat16), (first < second).astype(jnp.bfloat16))
        rank = jnp.sum(before * hot, axis=0, keepdims=True).astype(jnp.int32)
        found = places(ids, rank, chunks, experts, 0, lambda slots: (slots, tokens))
        for ref, value in zip(place, found):
            ref[...] = value
        ids = col_ids[...]
        hot = (lax.broadcasted_iota(jnp.int32, (tokens, experts), 1) == ids).astype(jnp.float32)
        before = dot((second < first).astype(jnp.bfloat16), hot.astype(jnp.bfloat16))
        rank = jnp.sum(before * hot, axis=1, keepdims=True).astype(jnp.int32)
        found = places(ids, rank, chunks, experts, 1, lambda slots: (tokens, slots))
        for ref, value in zip(place_back, found):
            ref[...] = value

    @pl.when(step < blocks)
    def _():
        for ref, at in zip(dealt, place):
            ref[...] = dot(at[...], stash[...]).astype(jnp.bfloat16)

    @pl.when(step >= blocks)
    def _():
        scaled = (gates[...] * out_grad[...].astype(jnp.float32)).astype(jnp.bfloat16)
        for ref, at in zip(dealt, place):
            ref[...] = dot(at[...], scaled).astype(jnp.bfloat16)


def deal(ids, gates, stash, out_grad, experts, chunks):
    tokens, width = stash.shape
    slots = [experts * HALVES * depth for depth in chunks]
    blocks = 4
    span = width // blocks
    outs = pl.pallas_call(
        functools.partial(deal_kernel, experts, chunks, blocks),
        grid=(2 * blocks,),
        in_specs=[
            pl.BlockSpec((1, tokens), lambda i: (0, 0)),
            pl.BlockSpec((tokens, 1), lambda i: (0, 0)),
            pl.BlockSpec((tokens, 1), lambda i: (0, 0)),
            pl.BlockSpec((tokens, span), lambda i: (0, jnp.minimum(i, blocks - 1))),
            pl.BlockSpec((tokens, span), lambda i: (0, jnp.maximum(i - blocks, 0))),
        ],
        out_specs=[pl.BlockSpec((count, span), lambda i: (0, i)) for count in slots]
        + [pl.BlockSpec((tokens, count), lambda i: (0, 0)) for count in slots],
        out_shape=[jax.ShapeDtypeStruct((count, 2 * width), jnp.bfloat16) for count in slots]
        + [jax.ShapeDtypeStruct((tokens, count), jnp.bfloat16) for count in slots],
        scratch_shapes=[pltpu.VMEM((count, tokens), jnp.bfloat16) for count in slots],
        compiler_params=pltpu.CompilerParams(vmem_limit_bytes=24 * MIB),
        cost_estimate=cost(4 * sum(slots) * tokens * width, 6 * sum(slots) * width),
        name="deal_rows",
    )(ids.reshape(1, tokens), ids, gates, stash, out_grad)
    return outs[: len(chunks)], outs[len(chunks) :]


def middle_kernel(steps, cuts, rows_ref, go, uo, do, gs, us, ds, *refs):
    backs, refs = refs[: len(cuts)], refs[len(cuts) :]
    hidden, deltas, held, joined, down, pre, tail, out, sems, out_sems = refs
    rows, width = out.shape
    units = go.shape[1]
    span = width // steps

    def block(k, base=0):
        return pl.ds(pl.multiple_of(base + k * span, span), span)

    def copies(k):
        at, late = block(k), block(k, width)
        pairs = [
            (rows_ref.at[:, at], held.at[:, at]),
            (rows_ref.at[:, late], held.at[:, late]),
            (do.at[:, at], down.at[pl.ds(0, units), at]),
            (ds.at[:, at], down.at[pl.ds(units, units), at]),
        ]
        for i, weight in enumerate((go, uo, gs, us)):
            pairs.append((weight.at[at, :], joined.at[at, pl.ds(i * units, units)]))
        return [
            pltpu.make_async_copy(src, dst, sems.at[i, k]) for i, (src, dst) in enumerate(pairs)
        ]

    @pl.loop(0, steps)
    def _(k):
        for copy in copies(k):
            copy.start()

    pre[...] = jnp.zeros_like(pre)
    tail[...] = jnp.zeros_like(tail)

    @pl.loop(0, steps)
    def _(k):
        for copy in copies(k):
            copy.wait()
        at, late = block(k), block(k, width)
        pre[...] += dot(held[:, at], joined[at, :])
        tail[...] += dot(held[:, late], down[:, at], NEXT_LAST)

    @pl.loop(0, rows // 16)
    def _(r):
        at = pl.ds(pl.multiple_of(r * 16, 16), 16)
        for core in range(CORES):
            gate = slice(2 * core * units, (2 * core + 1) * units)
            up = slice((2 * core + 1) * units, (2 * core + 2) * units)
            own = slice(core * units, (core + 1) * units)
            gate_pre, up_pre, grad = pre[at, gate], pre[at, up], tail[at, own]
            sigmoid_a = jax.nn.sigmoid(gate_pre)
            silu_a = gate_pre * sigmoid_a
            hidden[at, own] = (silu_a * up_pre).astype(jnp.bfloat16)
            deltas[at, gate] = (
                grad * up_pre * sigmoid_a * (1.0 + gate_pre * (1.0 - sigmoid_a))
            ).astype(jnp.bfloat16)
            deltas[at, up] = (grad * silu_a).astype(jnp.bfloat16)

    def leave(back, k, begin):
        return pltpu.make_async_copy(out.at[:, block(k)], back.at[:, block(k - begin)], out_sems.at[k])

    begin = 0
    ranges = []
    for back, cut in zip(backs, cuts):
        ranges.append((back, begin, begin + cut // span))
        begin += cut // span
    for back, begin, end in ranges:

        @pl.loop(begin, end)
        def _(k):
            out[:, block(k)] = dot(deltas[...], joined[block(k), :], NEXT_LAST).astype(jnp.bfloat16)
            leave(back, k, begin).start()

    for back, begin, end in ranges:

        @pl.loop(begin, end)
        def _(k):
            leave(back, k, begin).wait()


def middle(rows, own, sibling, cuts):
    count, width = rows.shape[0], rows.shape[1] // 2
    units = own[0].shape[1]
    steps = 8
    anywhere = pl.BlockSpec(memory_space=pl.ANY)
    whole = pl.BlockSpec(memory_space=pltpu.VMEM)
    outs = pl.pallas_call(
        functools.partial(middle_kernel, steps, cuts),
        in_specs=[anywhere] * 7,
        out_specs=[anywhere] * len(cuts) + [whole] * 2,
        out_shape=[jax.ShapeDtypeStruct((count, cut), jnp.bfloat16) for cut in cuts]
        + [
            jax.ShapeDtypeStruct((count, CORES * units), jnp.bfloat16),
            jax.ShapeDtypeStruct((count, 2 * CORES * units), jnp.bfloat16),
        ],
        scratch_shapes=[
            pltpu.VMEM((count, 2 * width), jnp.bfloat16),
            pltpu.VMEM((width, 2 * CORES * units), jnp.bfloat16),
            pltpu.VMEM((CORES * units, width), jnp.bfloat16),
            pltpu.VMEM((count, 2 * CORES * units), jnp.float32),
            pltpu.VMEM((count, CORES * units), jnp.float32),
            pltpu.VMEM((count, width), jnp.bfloat16),
            pltpu.SemaphoreType.DMA((8, steps)),
            pltpu.SemaphoreType.DMA((steps,)),
        ],
        compiler_params=pltpu.CompilerParams(vmem_limit_bytes=52 * MIB),
        cost_estimate=cost(10 * count * width * CORES * units, 30 * MIB),
        name="middle",
    )(rows, *own, *sibling)
    return outs[: len(cuts)], outs[-2], outs[-1]


def grads_kernel(number, added, *refs):
    tokens, grads, hidden, deltas = (refs[i * number : (i + 1) * number] for i in range(4))
    gate, up, down = refs[-3:]
    units = gate.shape[1]
    both = sum(dot(t[...], d[...], FIRST_FIRST) for t, d in zip(tokens, deltas))
    low = sum(dot(h[...], g[...], FIRST_FIRST) for h, g in zip(hidden, grads))
    parts = [both[:, :units], both[:, units:], low]
    if added:
        received = refs[4 * number : 4 * number + 3]
        parts = [part + ref[...].astype(jnp.float32) for part, ref in zip(parts, received)]
    for ref, part in zip((gate, up, down), parts):
        ref[...] = part.astype(jnp.bfloat16)


def weight_grads(rows, hidden, deltas, core, received=()):
    counts = [part.shape[0] for part in rows]
    width = rows[0].shape[1] // 2
    units = hidden[0].shape[1] // CORES
    steps = 8
    span = width // steps
    tall = pl.BlockSpec((span, units), lambda i: (i, 0))
    wide = pl.BlockSpec((units, span), lambda i: (0, i))
    return pl.pallas_call(
        functools.partial(grads_kernel, len(rows), len(received) > 0),
        grid=(steps,),
        in_specs=[pl.BlockSpec((count, span), lambda i: (0, i)) for count in counts]
        + [pl.BlockSpec((count, span), lambda i: (0, i + steps)) for count in counts]
        + [pl.BlockSpec((count, units), lambda i: (0, core)) for count in counts]
        + [pl.BlockSpec((count, 2 * units), lambda i: (0, core)) for count in counts]
        + [tall, tall, wide][: len(received)],
        out_specs=[tall, tall, wide],
        out_shape=[
            jax.ShapeDtypeStruct((width, units), jnp.bfloat16),
            jax.ShapeDtypeStruct((width, units), jnp.bfloat16),
            jax.ShapeDtypeStruct((units, width), jnp.bfloat16),
        ],
        compiler_params=pltpu.CompilerParams(vmem_limit_bytes=LIMIT),
        cost_estimate=cost(6 * sum(counts) * width * units, 16 * MIB),
        name="own_grads" if received else "sibling_grads",
    )(*rows, *rows, *hidden, *deltas, *received)


def body(stash, out_grad, expert_ids, gate_probs, w_gate, w_up, w_down):
    chips = lax.axis_size("chip")
    sections = lax.axis_size("section")
    tokens = stash.shape[1]
    experts = chips * CORES // SPLIT
    capacity = tokens * 3 // (2 * experts)
    own = (w_gate[0, 0], w_up[0, 0], w_down[0, 0])
    sibling = tuple(swap_cores(weight) for weight in own)
    (dealt,), (place_back,) = deal(
        expert_ids[0], gate_probs[0], stash[0], out_grad[0], experts, (capacity,)
    )
    dealt, sibling = lax.optimization_barrier((dealt, sibling))
    rows = over_chips(dealt)
    width = stash.shape[2]
    backs, hidden, deltas = middle(rows, own, sibling, (width * 3 // 4, width // 4))
    theirs = weight_grads([rows], [hidden], [deltas], 1)
    received = tuple(swap_cores(part) for part in theirs)

    def shift(returned):
        input_grad = dot(place_back, returned).astype(jnp.bfloat16)
        return input_grad, lambda value: lax.ppermute(
            value, "section", [(i, (i - 1) % sections) for i in range(sections)]
        )

    first = over_chips(backs[0])
    last, first = lax.optimization_barrier((backs[1], first))
    last = over_chips(last)
    first, move = shift(first)
    deltas, first = lax.optimization_barrier((deltas, first))
    first = move(first)
    grads = weight_grads([rows], [hidden], [deltas], 0, received)
    last, move = shift(last)
    last = move(last)
    prev_grad = jnp.concatenate([first, last], axis=1)
    return (prev_grad[None],) + tuple(grad[None, None] for grad in grads)


def solution(mesh):
    sections, devices = mesh.devices.shape
    fine = Mesh(mesh.devices.reshape(sections, devices // CORES, CORES), ("section", "chip", "core"))
    spec = P("section", ("chip", "core"))
    return jax.shard_map(
        body, mesh=fine, in_specs=(spec,) * 7, out_specs=(spec,) * 4, check_vma=False
    )
```
